32 devices in a mesh: groups: 2 (over x), lat: 8 (over z, y), lev: 2 (over core).
Axes of the slice: x: 2, y: 2, z: 4, core: 2. Of those that a mesh axis runs over, the one named last changes fastest.
Arguments:
- state: float32 [256, 128, 1024], P(('groups', 'lat'), None, 'lev'), parts along dimension 0, may hold values from -6 to 6
- humidity: bfloat16 [256, 128, 1024], P(('groups', 'lat'), None, 'lev'), parts along dimension 0, may hold values from -6 to 6
- sun_list: int32 [16, 2, 64], P(('groups', 'lat'), 'lev'), parts along dimension 0, may hold values from 0 to 63, as said below
- sun_count: int32 [16, 2], P(('groups', 'lat'), 'lev'), parts along dimension 0, may hold values from 0 to 64, as said below
- w_in: bfloat16 [256, 256], replicated, may hold values from -0.375 to 0.375
- w_mid: bfloat16 [256, 256], replicated, may hold values from -0.375 to 0.375
- w_out: bfloat16 [256, 128], replicated, may hold values from -0.375 to 0.375
Outputs:
- new_state: float32 [256, 128, 1024], P(('groups', 'lat'), None, 'lev'), parts along dimension 0
The draws below stay inside these ranges and needn't reach their ends.
There are 2 independent parts, one for each index of `groups`. The reference program is written for one: setup_inputs(seed, part) draws one part's arguments, and reference() takes and returns one part's arrays. A program takes and returns all parts, laid end to end along the dimension named above; an argument that names none is the same for every part. Nothing has to cross between parts.
Inputs may be any that keep to these rules, and one draw needn't show every extreme that they name: For every lat index i below 4 and lev index k, sun_count[i, k] + sun_count[i + 4, k] = 64, and sun_count[i, k] >= 32; the lat index 0 devices are fully sunlit. `sun_list`: each device's row is an ordering of its 64 blocks; its first sun_count entries are its sunlit blocks.
All inputs are finite; a program needn't handle non-finite values.
Results may differ from the reference program's by a relative error of at most 0.0024.
Values may be sent and summed in bfloat16 or wider, within the bound.
A program may use at most 128 MiB of HBM per device.

```python
import jax
import jax.numpy as jnp
from jax import lax

L = 128
H = 256
NLON = 1024
BLOCK = 128
NLAT = 128
NBLK = 64
N_LAT = 8
N_LEV = 2


def draw_sun_count(key, part):
    key = jax.random.fold_in(key, 11)
    half_lat = N_LAT // 2
    lowest = NBLK - max(NBLK // 8, 1)
    summer_side = jax.random.randint(key, (half_lat, N_LEV), lowest, NBLK + 1)
    summer_side = summer_side.at[0].set(NBLK)
    winter_side = NBLK - summer_side
    return jnp.concatenate([summer_side, winter_side], axis=0).astype(jnp.int32)


def draw_sun_list(key, part):
    key = jax.random.fold_in(key, 12)
    row_keys = jax.random.split(key, N_LAT * N_LEV)

    def one_ordering(row_key):
        return jax.random.permutation(row_key, NBLK)
    orderings = jax.vmap(one_ordering)(row_keys)
    return orderings.reshape(N_LAT, N_LEV, NBLK).astype(jnp.int32)


def shard_levels(own_key, extent, pieces, smallest, high):
    def one(position, blocks):
        steps = jax.random.uniform(jax.random.fold_in(jax.random.fold_in(own_key, 6), position), (blocks,), jnp.float32, smallest / len(pieces), high / len(pieces))
        return jnp.repeat(jnp.exp(steps), extent[position] // blocks).reshape((-1,) + (1,) * (len(extent) - position - 1))

    loudness = one(*pieces[0])
    for cut in pieces[1:]:
        loudness = loudness * one(*cut)
    return loudness


def gaussian(key, shape, scale, reach, cuts=(), kind=jnp.bfloat16):
    array = scale * jax.random.normal(key, shape, jnp.float32)
    if cuts:
        array = array * shard_levels(key, shape, cuts, -0.22, 0.18)
    return jnp.clip(array, -reach, reach).astype(kind)


def setup_inputs(seed: int = 0, part: int = 0) -> dict:
    arg_keys = jax.random.split(jax.random.key(seed), 8)
    part_keys = jax.random.split(jax.random.fold_in(arg_keys[7], part), 8)
    return {
        "state": gaussian(part_keys[0], (NLAT, L, NLON), 1.0, 6.0, ((0, 8), (2, 2)), jnp.float32),
        "humidity": gaussian(part_keys[1], (NLAT, L, NLON), 1.0, 6.0, ((0, 8), (2, 2))),
        "sun_list": draw_sun_list(jax.random.fold_in(jax.random.fold_in(arg_keys[7], part), 71), part),
        "sun_count": draw_sun_count(jax.random.fold_in(jax.random.fold_in(arg_keys[7], part), 71), part),
        "w_in": gaussian(arg_keys[4], (2 * L, H), (2 * L) ** -0.5, 0.375),
        "w_mid": gaussian(arg_keys[5], (H, H), H ** -0.5, 0.375),
        "w_out": gaussian(arg_keys[6], (H, L), H ** -0.5, 0.375),
    }


damping_strength = 10.0

def legendre_table(order_values, nlat):
    colatitude = jnp.pi * (jnp.arange(nlat, dtype=jnp.float32) + 0.5) / nlat
    cosines = jnp.cos(colatitude)
    sines = jnp.sin(colatitude)
    weights = jnp.pi / nlat * sines
    order_float = order_values.astype(jnp.float32)[:, None]
    indices = jnp.arange(1, nlat, dtype=jnp.float32)
    log_steps = jnp.log((2.0 * indices + 1.0) / (2.0 * indices))
    cumulative = jnp.concatenate([jnp.zeros((1,), jnp.float32), jnp.cumsum(log_steps)])
    matches = jnp.arange(nlat, dtype=jnp.int32)[None, :] == order_values[:, None]
    picked = lax.optimization_barrier(jnp.sum(jnp.where(matches, cumulative[None, :], 0.0), axis=1))
    diagonal = jnp.exp(0.5 * jnp.log(0.5) + 0.5 * picked[:, None] + order_float * jnp.log(sines)[None, :])
    order_column = order_values[:, None]

    def recurrence(state_pair, degree):
        previous, earlier = state_pair
        degree_float = degree.astype(jnp.float32)
        first_step = jnp.sqrt(2.0 * order_float + 3.0) * cosines[None, :] * previous
        factor_now = jnp.sqrt((4.0 * degree_float ** 2 - 1.0) / jnp.maximum(degree_float ** 2 - order_float ** 2, 1.0))
        lower_degree = degree_float - 1.0
        factor_back = jnp.sqrt(jnp.maximum(lower_degree ** 2 - order_float ** 2, 0.0) / jnp.maximum(4.0 * lower_degree ** 2 - 1.0, 1.0))
        general = factor_now * (cosines[None, :] * previous - factor_back * earlier)
        value = jnp.where(degree == order_column, diagonal, jnp.where(degree == order_column + 1, first_step, jnp.where(degree > order_column + 1, general, 0.0)))
        return ((value, previous), value)
    start = jnp.zeros((order_values.shape[0], nlat), jnp.float32)
    unused, values = lax.scan(recurrence, (start, start), jnp.arange(nlat, dtype=jnp.int32), unroll=8)
    return (jnp.transpose(values, (1, 2, 0)), weights)

def damping_factors(nlat):
    degrees = jnp.arange(nlat, dtype=jnp.float32)
    scaled = degrees * (degrees + 1.0) / ((nlat - 1.0) * nlat)
    return 1.0 / (1.0 + damping_strength * scaled ** 2) - 1.0

def radiation_net(blocks, w_in, w_mid, w_out):
    first = jnp.einsum('bfc,fh->bhc', blocks.astype(jnp.float32), w_in.astype(jnp.float32))
    hidden_one = jax.nn.silu(first).astype(jnp.bfloat16)
    second = jnp.einsum('bhc,hk->bkc', hidden_one.astype(jnp.float32), w_mid.astype(jnp.float32))
    hidden_two = jax.nn.silu(second).astype(jnp.bfloat16)
    output = jnp.einsum('bkc,kl->blc', hidden_two.astype(jnp.float32), w_out.astype(jnp.float32))
    return output.astype(jnp.bfloat16)

def reference(state, humidity, sun_list, sun_count, w_in, w_mid, w_out):
    nlat, levels, nlon = state.shape
    lat_dev = nlat // N_LAT
    half_lon = nlon // N_LEV
    per_row = half_lon // BLOCK
    nblk = lat_dev * per_row
    total_blocks = N_LAT * N_LEV * nblk
    state_low = state.astype(jnp.bfloat16)

    def to_blocks(field):
        shaped = field.reshape(N_LAT, lat_dev, levels, N_LEV, per_row, BLOCK)
        return shaped.transpose(0, 3, 1, 4, 2, 5).reshape(total_blocks, levels, BLOCK)
    profiles = jnp.concatenate([to_blocks(state_low), to_blocks(humidity)], axis=1)
    device_base = (jnp.arange(N_LAT * N_LEV, dtype=jnp.int32) * nblk).reshape(N_LAT, N_LEV, 1)
    global_ids = (sun_list.astype(jnp.int32) + device_base).reshape(-1)
    lit_mask = (jnp.arange(nblk, dtype=jnp.int32)[None, None, :] < sun_count[:, :, None]).reshape(-1)
    ordering = jnp.argsort(jnp.where(lit_mask, 0, 1).astype(jnp.int32), stable=True)
    lit_ids = global_ids[ordering[:total_blocks // 2]].reshape(N_LAT, total_blocks // (2 * N_LAT))

    def network_rows(row_ids):
        return radiation_net(profiles[row_ids], w_in, w_mid, w_out)
    lit_heating = lax.map(network_rows, lit_ids)
    heating_blocks = jnp.zeros((total_blocks, levels, BLOCK), jnp.float32)
    heating_blocks = heating_blocks.at[lit_ids.reshape(-1)].set(lit_heating.reshape(-1, levels, BLOCK).astype(jnp.float32))
    heating_grid = heating_blocks.reshape(N_LAT, N_LEV, lat_dev, per_row, levels, BLOCK)
    heating_grid = heating_grid.transpose(0, 2, 4, 1, 3, 5).reshape(nlat, levels, nlon)
    longitudes = jnp.arange(nlon, dtype=jnp.int32)
    wavenumbers = jnp.arange(nlat, dtype=jnp.int32)
    phase = longitudes[:, None] * wavenumbers[None, :] % nlon
    angle = phase.astype(jnp.float32) * (2.0 * jnp.pi / nlon)
    forward_table = jnp.concatenate([jnp.cos(angle), -jnp.sin(angle)], axis=1).astype(jnp.bfloat16)
    multiplicity = jnp.where(wavenumbers == 0, 1.0, 2.0).astype(jnp.float32)
    inverse_table = jnp.concatenate([jnp.cos(angle).T * multiplicity[:, None], -jnp.sin(angle).T * multiplicity[:, None]], axis=0).astype(jnp.bfloat16)

    def forward_row(row):
        return (jnp.dot(row, forward_table, preferred_element_type=jnp.float32) / nlon).astype(jnp.bfloat16)
    fourier = lax.map(forward_row, state_low)
    real_part = fourier[:, :, :nlat]
    imag_part = fourier[:, :, nlat:]
    table, weights = legendre_table(jnp.arange(nlat, dtype=jnp.int32), nlat)
    analysis = (table * weights[None, :, None]).astype(jnp.bfloat16).astype(jnp.float32)
    synthesis = table.astype(jnp.bfloat16).astype(jnp.float32)
    damping = damping_factors(nlat)
    highest = lax.Precision.HIGHEST

    def through_spectral(part):
        spectral = jnp.einsum('jlm,mjn->mnl', part.astype(jnp.float32), analysis, precision=highest)
        damped = (spectral * damping[None, :, None]).astype(jnp.bfloat16)
        back = jnp.einsum('mnl,mjn->jlm', damped.astype(jnp.float32), synthesis, precision=highest)
        return back.astype(jnp.bfloat16)
    back_real = through_spectral(real_part)
    back_imag = through_spectral(imag_part)
    back_both = jnp.concatenate([back_real, back_imag], axis=2)

    def inverse_row(row):
        return jnp.dot(row, inverse_table, preferred_element_type=jnp.float32)
    increment = lax.map(inverse_row, back_both)
    return state + heating_grid + increment
```

```python
import jax
import jax.numpy as jnp
from jax import lax
from jax.experimental import pallas as pl
from jax.experimental.pallas import tpu as pltpu
from jax.sharding import PartitionSpec as P

BLOCK = 128


damping_strength = 10.0


def legendre_rows(order, cosines, diagonal_ref, out_ref, nlat):
    order_float = order.astype(jnp.float32)
    order_square = order_float * order_float

    def step(degree, pair):
        previous, earlier = pair
        degree_float = degree.astype(jnp.float32)
        square = degree_float * degree_float
        lower = degree_float - 1.0
        lower_square = lower * lower
        factor_now = jnp.sqrt((4.0 * square - 1.0) / jnp.maximum(square - order_square, 1.0))
        factor_back = jnp.sqrt(
            jnp.maximum(lower_square - order_square, 0.0)
            / jnp.maximum(4.0 * lower_square - 1.0, 1.0)
        )
        general = factor_now * (cosines * previous - factor_back * earlier)
        value = jnp.where(degree == order, diagonal_ref[...], jnp.where(degree > order, general, 0.0))
        out_ref[degree] = value
        return value, previous

    start = diagonal_ref[...] * 0.0
    lax.fori_loop(0, nlat, step, (start, start), unroll=8)


def legendre_kernel(cosine_ref, diagonal_ref, out_ref):
    nlat = out_ref.shape[0]
    orders = diagonal_ref.shape[0]
    order = lax.axis_index("lat") * orders + lax.broadcasted_iota(jnp.int32, diagonal_ref.shape, 0)
    legendre_rows(order, cosine_ref[...], diagonal_ref, out_ref, nlat)


def legendre_inputs(order_values, nlat):
    colatitude = jnp.pi * (jnp.arange(nlat, dtype=jnp.float32) + 0.5) / nlat
    cosines = jnp.cos(colatitude)
    sines = jnp.sin(colatitude)
    weights = jnp.pi / nlat * sines
    order_float = order_values.astype(jnp.float32)[:, None]
    indices = jnp.arange(1, nlat, dtype=jnp.float32)
    log_steps = jnp.log((2.0 * indices + 1.0) / (2.0 * indices))
    below = jnp.arange(1, nlat, dtype=jnp.int32)[None, :] <= order_values[:, None]
    picked = jnp.sum(jnp.where(below, log_steps[None, :], 0.0), axis=1)
    diagonal = jnp.exp(
        0.5 * jnp.log(0.5) + 0.5 * picked[:, None] + order_float * jnp.log(sines)[None, :]
    )
    return cosines, weights, diagonal


def legendre_table(order_values, nlat):
    cosines, weights, diagonal = legendre_inputs(order_values, nlat)
    table = pl.pallas_call(
        legendre_kernel,
        out_shape=jax.ShapeDtypeStruct((nlat,) + diagonal.shape, jnp.float32),
        compiler_params=pltpu.CompilerParams(vmem_limit_bytes=48 * 2**20),
    )(jnp.broadcast_to(cosines[None, :], diagonal.shape), diagonal)
    return table, weights


def damping_factors(nlat):
    degrees = jnp.arange(nlat, dtype=jnp.float32)
    scaled = degrees * (degrees + 1.0) / ((nlat - 1.0) * nlat)
    return 1.0 / (1.0 + damping_strength * scaled**2) - 1.0


def radiation_net(blocks, w_in, w_mid, w_out):
    first = jnp.einsum("bfc,fh->bhc", blocks, w_in, preferred_element_type=jnp.float32)
    hidden_one = jax.nn.silu(first).astype(jnp.bfloat16)
    second = jnp.einsum("bhc,hk->bkc", hidden_one, w_mid, preferred_element_type=jnp.float32)
    hidden_two = jax.nn.silu(second).astype(jnp.bfloat16)
    output = jnp.einsum("bkc,kl->blc", hidden_two, w_out, preferred_element_type=jnp.float32)
    return output.astype(jnp.bfloat16)


def select_rows(row_ids, source):
    count = source.shape[0]
    picker = (row_ids[:, None] == jnp.arange(count, dtype=jnp.int32)[None, :]).astype(jnp.bfloat16)
    return jnp.einsum("sb,bfc->sfc", picker, source, preferred_element_type=jnp.float32).astype(
        jnp.bfloat16
    )


def local(state, humidity, sun_list, sun_count, w_in, w_mid, w_out):
    lat_dev, levels, half_lon = state.shape
    per_row = half_lon // BLOCK
    nblk = lat_dev * per_row
    lat_size = lax.axis_size("lat")
    lev_size = lax.axis_size("lev")
    nlat = lat_dev * lat_size
    nlon = half_lon * lev_size
    state_low = state.astype(jnp.bfloat16)

    def to_blocks(field):
        shaped = field.reshape(lat_dev, levels, per_row, BLOCK)
        return shaped.transpose(0, 2, 1, 3).reshape(nblk, levels, BLOCK)

    profiles = jnp.concatenate([to_blocks(state_low), to_blocks(humidity)], axis=1)
    listing = sun_list[0, 0]
    lit_count = sun_count[0, 0]
    positions = jnp.arange(nblk, dtype=jnp.int32)
    listed_heating = radiation_net(select_rows(listing, profiles), w_in, w_mid, w_out)
    placer = (listing[None, :] == positions[:, None]) & (positions[None, :] < lit_count)
    heating_blocks = jnp.einsum(
        "pb,blc->plc",
        placer.astype(jnp.bfloat16),
        listed_heating,
        preferred_element_type=jnp.float32,
    )
    heating_grid = heating_blocks.reshape(lat_dev, per_row, levels, BLOCK).transpose(0, 2, 1, 3)
    heating_grid = heating_grid.reshape(lat_dev, levels, half_lon)
    longitudes = lax.axis_index("lev") * half_lon + jnp.arange(half_lon, dtype=jnp.int32)
    wavenumbers = jnp.arange(nlat, dtype=jnp.int32)
    phase = longitudes[:, None] * wavenumbers[None, :] % nlon
    angle = phase.astype(jnp.float32) * (2.0 * jnp.pi / nlon)
    cos_table = jnp.cos(angle)
    sin_table = jnp.sin(angle)
    forward_tables = jnp.stack([cos_table, -sin_table]).astype(jnp.bfloat16)
    selected = forward_tables
    fourier = lax.psum_scatter(
        jnp.einsum("ilx,rxm->riml", state_low, selected, preferred_element_type=jnp.float32) / nlon,
        "lev",
        scatter_dimension=0,
        tiled=True,
    ).astype(jnp.bfloat16)
    by_wave = lax.all_to_all(fourier, "lat", split_axis=2, concat_axis=1, tiled=True)
    owned = lax.axis_index("lat") * lat_dev + jnp.arange(lat_dev, dtype=jnp.int32)
    table, weights = legendre_table(owned, nlat)
    analysis = (table * weights[None, None, :]).astype(jnp.bfloat16)
    synthesis = table.astype(jnp.bfloat16)
    spectral = jnp.einsum("rjml,nmj->rmnl", by_wave, analysis, preferred_element_type=jnp.float32)
    damped = (spectral * damping_factors(nlat)[None, None, :, None]).astype(jnp.bfloat16)
    back_four = jnp.einsum(
        "rmnl,nmj->rjml", damped, synthesis, preferred_element_type=jnp.float32
    ).astype(jnp.bfloat16)
    by_lat = lax.all_to_all(back_four, "lat", split_axis=1, concat_axis=2, tiled=True)
    multiplicity = jnp.where(wavenumbers == 0, 1.0, 2.0).astype(jnp.float32)
    inverse_tables = jnp.stack(
        [cos_table.T * multiplicity[:, None], -sin_table.T * multiplicity[:, None]]
    ).astype(jnp.bfloat16)
    selected = inverse_tables
    increment = jnp.einsum(
        "riml,rmx->ilx",
        lax.all_gather(by_lat, "lev", axis=0, tiled=True),
        selected,
        preferred_element_type=jnp.float32,
    )
    return state + heating_grid + increment


def solution(mesh):
    return jax.shard_map(
        local,
        mesh=mesh,
        in_specs=(
            P(("groups", "lat"), None, "lev"),
            P(("groups", "lat"), None, "lev"),
            P(("groups", "lat"), "lev", None),
            P(("groups", "lat"), "lev"),
            P(),
            P(),
            P(),
        ),
        out_specs=P(("groups", "lat"), None, "lev"),
        check_vma=False,
    )
```

```python
import functools

import jax
import jax.numpy as jnp
from jax import lax
from jax.experimental import pallas as pl
from jax.experimental.pallas import tpu as pltpu
from jax.sharding import PartitionSpec as P

BLOCK = 128
MESH = pl.DeviceIdType.MESH
MIB = 2**20

damping_strength = 10.0


def legendre_inputs(order_values, nlat):
    colatitude = jnp.pi * (jnp.arange(nlat, dtype=jnp.float32) + 0.5) / nlat
    cosines = jnp.cos(colatitude)
    sines = jnp.sin(colatitude)
    weights = jnp.pi / nlat * sines
    order_float = order_values.astype(jnp.float32)[:, None]
    indices = jnp.arange(1, nlat, dtype=jnp.float32)
    log_steps = jnp.log((2.0 * indices + 1.0) / (2.0 * indices))
    below = jnp.arange(1, nlat, dtype=jnp.int32)[None, :] <= order_values[:, None]
    picked = jnp.sum(jnp.where(below, log_steps[None, :], 0.0), axis=1)
    diagonal = jnp.exp(
        0.5 * jnp.log(0.5) + 0.5 * picked[:, None] + order_float * jnp.log(sines)[None, :]
    )
    return cosines, weights, diagonal


def damping_factors(nlat):
    degrees = jnp.arange(nlat, dtype=jnp.float32)
    scaled = degrees * (degrees + 1.0) / ((nlat - 1.0) * nlat)
    return 1.0 / (1.0 + damping_strength * scaled**2) - 1.0


def silu(value):
    half = 0.5 * value
    return half + half * jnp.tanh(half)


def dot(left, right, contract):
    return lax.dot_general(left, right, (contract, ((), ())), preferred_element_type=jnp.float32)


def kernel(
    lat_size,
    scale,
    table_ref,
    cosine_ref,
    diagonal_ref,
    weight_ref,
    damping_ref,
    lit_ref,
    w_in_ref,
    w_mid_ref,
    w_out_ref,
    state_ref,
    humidity_ref,
    out_ref,
    grid,
    humid,
    partial,
    from_sibling,
    to_wave,
    by_wave,
    degrees,
    analysis,
    synthesis,
    to_lat,
    by_lat,
    sibling_part,
    wt_in,
    wt_mid,
    wt_out,
    state_sem,
    humid_sem,
    out_sem,
    pair_send,
    pair_recv,
    wave_send,
    wave_recv,
    lat_send,
    lat_recv,
    share_send,
    share_recv,
):
    rows, levels, lons = grid.shape
    nlat = lat_size * rows
    chunk = rows * rows
    me = lax.axis_index("lat")
    sibling = 1 - lax.axis_index("lev")

    loads = [
        pltpu.make_async_copy(state_ref.at[j], grid.at[j], state_sem.at[j]) for j in range(rows)
    ]
    for load in loads:
        load.start()
    humid_load = pltpu.make_async_copy(humidity_ref, humid, humid_sem)
    humid_load.start()

    barrier = pltpu.get_barrier_semaphore()
    for step in range(1, lat_size):
        pl.semaphore_signal(
            barrier,
            inc=1,
            device_id={"lat": lax.rem(me + step, lat_size)},
            device_id_type=MESH,
        )
    pl.semaphore_signal(barrier, inc=1, device_id={"lev": sibling}, device_id_type=MESH)

    for j in range(rows):
        loads[j].wait()
        sums = dot(table_ref[...], grid[j].astype(jnp.bfloat16), ((1,), (1,))) * scale
        partial[0, pl.ds(j, nlat, stride=rows), :] = sums[:nlat]
        partial[1, pl.ds(j, nlat, stride=rows), :] = sums[nlat:]

    pl.semaphore_wait(barrier, lat_size)

    middle = lat_size // 2
    order = sorted(range(1, lat_size), key=lambda step: abs(step - middle)) + [0]

    def owner(step):
        return lax.rem(me + step, lat_size)

    def source(step):
        return lax.rem(me + lat_size - step, lat_size)

    def chunk_rows(index):
        return pl.ds(pl.multiple_of(index * chunk, chunk), chunk)

    pairs = {}
    for step in order:
        place = chunk_rows(owner(step))
        pairs[step] = pltpu.make_async_remote_copy(
            src_ref=partial.at[1, place],
            dst_ref=from_sibling.at[place],
            send_sem=pair_send.at[step],
            recv_sem=pair_recv.at[step],
            device_id={"lev": sibling},
            device_id_type=MESH,
        )
        pairs[step].start()

    waves = {}
    for step in order:
        place = chunk_rows(owner(step))
        pairs[step].wait_recv()
        whole = (partial[0, place] + from_sibling[place]).astype(jnp.bfloat16)
        if step == 0:
            by_wave[me] = whole
            continue
        to_wave[place] = whole
        waves[step] = pltpu.make_async_remote_copy(
            src_ref=to_wave.at[place],
            dst_ref=by_wave.at[me],
            send_sem=wave_send.at[step],
            recv_sem=wave_recv.at[step],
            device_id={"lat": owner(step)},
            device_id_type=MESH,
        )
        waves[step].start()

    orders = me * rows + lax.broadcasted_iota(jnp.int32, diagonal_ref.shape, 0)
    order_float = orders.astype(jnp.float32)
    order_square = order_float * order_float
    cosines = cosine_ref[...]
    wide, span, lanes = degrees.shape[0], degrees.shape[1] // rows, degrees.shape[2]

    def recurrence(base, index, pair):
        previous, earlier = pair
        degree = base + index
        degree_float = degree.astype(jnp.float32)
        square = degree_float * degree_float
        lower = degree_float - 1.0
        lower_square = lower * lower
        factor_now = jnp.sqrt((4.0 * square - 1.0) / jnp.maximum(square - order_square, 1.0))
        factor_back = jnp.sqrt(
            jnp.maximum(lower_square - order_square, 0.0)
            / jnp.maximum(4.0 * lower_square - 1.0, 1.0)
        )
        general = factor_now * (cosines * previous - factor_back * earlier)
        value = jnp.where(degree == orders, diagonal_ref[...], jnp.where(degree > orders, general, 0.0))
        place = pl.ds(pl.multiple_of(index * rows, rows), rows)
        for part in range(wide):
            degrees[part, place] = value[:, part * lanes : (part + 1) * lanes]
        return value, previous

    pair = (diagonal_ref[...] * 0.0, diagonal_ref[...] * 0.0)
    for base in range(0, nlat, span):
        pair = lax.fori_loop(0, span, functools.partial(recurrence, base), pair, unroll=4)

        @pl.loop(0, rows)
        def _(m):
            picked = jnp.concatenate(
                [degrees[part, pl.ds(m, span, stride=rows), :] for part in range(wide)], axis=1
            )
            analysis[m, base : base + span, :] = (picked * weight_ref[...]).astype(jnp.bfloat16)
            synthesis[m, :, base : base + span] = picked.T.astype(jnp.bfloat16)

    wt_in[...] = w_in_ref[...].astype(jnp.float32).T.astype(jnp.bfloat16)
    wt_mid[...] = w_mid_ref[...].astype(jnp.float32).T.astype(jnp.bfloat16)
    wt_out[...] = w_out_ref[...].astype(jnp.float32).T.astype(jnp.bfloat16)
    humid_load.wait()

    def network_row(j):
        profile = jnp.concatenate([grid[j].astype(jnp.bfloat16), humid[j]], axis=0)
        first = silu(dot(wt_in[...], profile, ((1,), (0,)))).astype(jnp.bfloat16)
        second = silu(dot(wt_mid[...], first, ((1,), (0,)))).astype(jnp.bfloat16)
        heating = dot(wt_out[...], second, ((1,), (0,))).astype(jnp.bfloat16).astype(jnp.float32)
        grid[j] = grid[j] + jnp.where(lit_ref[pl.ds(j, 1), :] > 0.5, heating, 0.0)

    early = rows // 2
    pl.loop(0, early)(network_row)

    for step in order[:-1]:
        waves[step].wait_recv()

    @pl.loop(0, rows)
    def _(m):
        place = pl.ds(pl.multiple_of(m * rows, rows), rows)
        fourier = by_wave[:, place, :].reshape(nlat, levels)
        spectral = dot(analysis[m], fourier, ((1,), (0,)))
        damped = (spectral * damping_ref[...]).astype(jnp.bfloat16)
        back = dot(synthesis[m], damped, ((1,), (0,)))
        doubled = jnp.where(me * rows + m == 0, 1.0, 2.0)
        to_lat[:, place, :] = (back * doubled).astype(jnp.bfloat16).reshape(lat_size, rows, levels)

    lats = {}
    for step in order[:-1]:
        lats[step] = pltpu.make_async_remote_copy(
            src_ref=to_lat.at[owner(step)],
            dst_ref=by_lat.at[me],
            send_sem=lat_send.at[step],
            recv_sem=lat_recv.at[step],
            device_id={"lat": owner(step)},
            device_id_type=MESH,
        )
        lats[step].start()
    by_lat[me] = to_lat[me]

    pl.loop(early, rows)(network_row)

    for step in order[:-1]:
        waves[step].wait_send()
    for step in order:
        pairs[step].wait_send()

    shares = {}
    arrival = [0] + order[:-1][::-1]
    for step in arrival:
        if step:
            lats[step].wait_recv()
        origin = source(step)
        shares[step] = pltpu.make_async_remote_copy(
            src_ref=by_lat.at[origin],
            dst_ref=sibling_part.at[origin],
            send_sem=share_send.at[step],
            recv_sem=share_recv.at[step],
            device_id={"lev": sibling},
            device_id_type=MESH,
        )
        shares[step].start()
        partial[0, chunk_rows(origin)] = by_lat[origin].astype(jnp.float32)
    for step in arrival:
        origin = source(step)
        shares[step].wait_recv()
        partial[1, chunk_rows(origin)] = sibling_part[origin].astype(jnp.float32)

    stores = [
        pltpu.make_async_copy(grid.at[j], out_ref.at[j], out_sem.at[j]) for j in range(rows)
    ]
    for j in range(rows):
        own = partial[0, pl.ds(j, nlat, stride=rows), :]
        other = partial[1, pl.ds(j, nlat, stride=rows), :]
        both = jnp.concatenate([own, other], axis=0).astype(jnp.bfloat16)
        grid[j] = grid[j] + dot(both, table_ref[...], ((0,), (0,)))
        stores[j].start()

    for step in order[:-1]:
        lats[step].wait_send()
    for step in arrival:
        shares[step].wait_send()
    for store in stores:
        store.wait()


def local(state, humidity, sun_list, sun_count, w_in, w_mid, w_out):
    rows, levels, half_lon = state.shape
    per_row = half_lon // BLOCK
    nblk = rows * per_row
    lat_size = lax.axis_size("lat")
    lev_size = lax.axis_size("lev")
    nlat = rows * lat_size
    nlon = half_lon * lev_size
    lev = lax.axis_index("lev")

    row = lax.broadcasted_iota(jnp.int32, (2 * nlat, half_lon), 0)
    longitude = lev * half_lon + lax.broadcasted_iota(jnp.int32, (2 * nlat, half_lon), 1)
    second = row >= nlat
    wavenumber = jnp.where(second, row - nlat, row)
    imaginary = second != (lev == 1)
    turned = longitude * wavenumber + jnp.where(imaginary, nlon // 4, 0)
    angle = (turned % nlon).astype(jnp.float32) * (2.0 * jnp.pi / nlon)
    table = jnp.cos(angle).astype(jnp.bfloat16)

    owned = lax.axis_index("lat") * rows + jnp.arange(rows, dtype=jnp.int32)
    cosines, weights, diagonal = legendre_inputs(owned, nlat)
    damping = jnp.broadcast_to(damping_factors(nlat)[:, None], (nlat, levels))
    positions = jnp.arange(nblk, dtype=jnp.int32)
    lit = jnp.any(
        (sun_list[0, 0][None, :] == positions[:, None]) & (positions[None, :] < sun_count[0, 0]),
        axis=1,
    )
    lit = jnp.repeat(lit.astype(jnp.float32).reshape(rows, per_row), BLOCK, axis=1)

    chunk = rows * rows
    span = min(nlat, 128)
    vmem = pl.BlockSpec(memory_space=pltpu.VMEM)
    hbm = pl.BlockSpec(memory_space=pl.ANY)
    dma = pltpu.SemaphoreType.DMA
    low = jnp.bfloat16
    return pl.pallas_call(
        functools.partial(kernel, lat_size, 1.0 / nlon),
        out_shape=jax.ShapeDtypeStruct(state.shape, jnp.float32),
        in_specs=[vmem] * 9 + [hbm] * 2,
        out_specs=hbm,
        scratch_shapes=[
            pltpu.VMEM(state.shape, jnp.float32),
            pltpu.VMEM(state.shape, low),
            pltpu.VMEM((2, nlat * rows, levels), jnp.float32),
            pltpu.VMEM((nlat * rows, levels), jnp.float32),
            pltpu.VMEM((nlat * rows, levels), low),
            pltpu.VMEM((lat_size, chunk, levels), low),
            pltpu.VMEM((nlat // span, span * rows, span), jnp.float32),
            pltpu.VMEM((rows, nlat, nlat), low),
            pltpu.VMEM((rows, nlat, nlat), low),
            pltpu.VMEM((lat_size, chunk, levels), low),
            pltpu.VMEM((lat_size, chunk, levels), low),
            pltpu.VMEM((lat_size, chunk, levels), low),
            pltpu.VMEM(w_in.shape[::-1], low),
            pltpu.VMEM(w_mid.shape[::-1], low),
            pltpu.VMEM(w_out.shape[::-1], low),
            dma((rows,)),
            dma,
            dma((rows,)),
        ]
        + [dma((lat_size,))] * 8,
        compiler_params=pltpu.CompilerParams(
            collective_id=0, has_side_effects=True, vmem_limit_bytes=58 * MIB
        ),
    )(
        table,
        jnp.broadcast_to(cosines[None, :], diagonal.shape),
        diagonal,
        jnp.broadcast_to(weights[None, :], (span, nlat)),
        damping,
        lit,
        w_in,
        w_mid,
        w_out,
        state,
        humidity,
    )


def solution(mesh):
    return jax.shard_map(
        local,
        mesh=mesh,
        in_specs=(
            P(("groups", "lat"), None, "lev"),
            P(("groups", "lat"), None, "lev"),
            P(("groups", "lat"), "lev", None),
            P(("groups", "lat"), "lev"),
            P(),
            P(),
            P(),
        ),
        out_specs=P(("groups", "lat"), None, "lev"),
        check_vma=False,
    )
```

```python
import functools
import math

import jax
import jax.numpy as jnp
from jax import lax
from jax.experimental import pallas as pl
from jax.experimental.pallas import tpu as pltpu
from jax.sharding import PartitionSpec as P

BLOCK = 128
MESH = pl.DeviceIdType.MESH
MIB = 2**20

damping_strength = 10.0


def sine(angle):
    square = angle * angle
    series = 1.6059044e-10
    for term in (-2.5052108e-8, 2.7557319e-6, -1.9841270e-4, 8.3333333e-3, -0.16666667):
        series = series * square + term
    return angle + angle * square * series


def iota(shape, dimension):
    return lax.broadcasted_iota(jnp.int32, shape, dimension)


def silu(value):
    half = 0.5 * value
    return half + half * jnp.tanh(half)


def dot(left, right, contract):
    return lax.dot_general(left, right, (contract, ((), ())), preferred_element_type=jnp.float32)


def kernel(
    lat_size,
    lev_size,
    count_ref,
    list_ref,
    w_in_ref,
    w_mid_ref,
    w_out_ref,
    state_ref,
    humidity_ref,
    out_ref,
    back_ref,
    table_ref,
    grid,
    humid,
    partial,
    from_sibling,
    to_wave,
    by_wave,
    diagonal_ref,
    damping_ref,
    lit_ref,
    degrees,
    analysis,
    synthesis,
    to_lat,
    by_lat,
    sibling_part,
    wt_in,
    wt_mid,
    wt_out,
    state_sem,
    humid_sem,
    out_sem,
    pair_send,
    pair_recv,
    wave_send,
    wave_recv,
    lat_send,
    lat_recv,
    share_send,
    share_recv,
):
    rows, levels, lons = grid.shape
    nlat = lat_size * rows
    chunk = rows * rows
    me = lax.axis_index("lat")
    sibling = 1 - lax.axis_index("lev")

    loads = [
        pltpu.make_async_copy(state_ref.at[j], grid.at[j], state_sem.at[j]) for j in range(rows)
    ]
    for load in loads:
        load.start()
    humid_load = pltpu.make_async_copy(humidity_ref, humid, humid_sem)
    humid_load.start()

    barrier = pltpu.get_barrier_semaphore()
    for step in range(1, lat_size):
        pl.semaphore_signal(
            barrier,
            inc=1,
            device_id={"lat": lax.rem(me + step, lat_size)},
            device_id_type=MESH,
        )
    pl.semaphore_signal(barrier, inc=1, device_id={"lev": sibling}, device_id_type=MESH)

    lev = lax.axis_index("lev")
    nlon = lons * lev_size
    strip = min(nlat, 128)
    for half in range(2):
        turn = jnp.where(lev == half, 0, nlon // 4)
        for base in range(0, nlat, strip):
            wavenumber = base + iota((strip, lons), 0)
            longitude = lev * lons + iota((strip, lons), 1)
            turned = longitude * wavenumber + turn
            phase = turned & (nlon - 1) if nlon & (nlon - 1) == 0 else turned % nlon
            fold = nlon // 4 - jnp.minimum(phase, nlon - phase)
            values = sine(fold.astype(jnp.float32) * (2.0 * math.pi / nlon))
            place = half * nlat + base
            table_ref[place : place + strip, :] = values.astype(jnp.bfloat16)

    for j in range(0, rows, 2):
        loads[j].wait()
        loads[j + 1].wait()
        two = grid[j : j + 2].astype(jnp.bfloat16).reshape(2 * levels, lons)
        sums = dot(table_ref[...], two, ((1,), (1,))) * (1.0 / nlon)
        for part in range(2):
            for row in range(2):
                partial[part, pl.ds(j + row, nlat, stride=rows), :] = sums[
                    part * nlat : (part + 1) * nlat, row * levels : (row + 1) * levels
                ]

    pl.semaphore_wait(barrier, lat_size)

    middle = lat_size // 2
    order = sorted(range(1, lat_size), key=lambda step: abs(step - middle)) + [0]

    def owner(step):
        return lax.rem(me + step, lat_size)

    def source(step):
        return lax.rem(me + lat_size - step, lat_size)

    def chunk_rows(index):
        return pl.ds(pl.multiple_of(index * chunk, chunk), chunk)

    pairs = {}
    for step in order:
        place = chunk_rows(owner(step))
        pairs[step] = pltpu.make_async_remote_copy(
            src_ref=partial.at[1, place],
            dst_ref=from_sibling.at[place],
            send_sem=pair_send.at[step],
            recv_sem=pair_recv.at[step],
            device_id={"lev": sibling},
            device_id_type=MESH,
        )
        pairs[step].start()

    waves = {}
    for step in order:
        place = chunk_rows(owner(step))
        pairs[step].wait_recv()
        whole = (partial[0, place] + from_sibling[place]).astype(jnp.bfloat16)
        if step == 0:
            by_wave[me] = whole
            continue
        to_wave[place] = whole
        waves[step] = pltpu.make_async_remote_copy(
            src_ref=to_wave.at[place],
            dst_ref=by_wave.at[me],
            send_sem=wave_send.at[step],
            recv_sem=wave_recv.at[step],
            device_id={"lat": owner(step)},
            device_id_type=MESH,
        )
        waves[step].start()

    orders = me * rows + iota(diagonal_ref.shape, 0)
    order_float = orders.astype(jnp.float32)
    order_square = order_float * order_float
    place = iota(diagonal_ref.shape, 1)
    cosines = sine((nlat - 1 - 2 * place).astype(jnp.float32) * (0.5 * math.pi / nlat))
    near = jnp.minimum(2 * place + 1, 2 * nlat - 1 - 2 * place).astype(jnp.float32)
    sines = sine(near * (0.5 * math.pi / nlat))
    weights = (sines * (math.pi / nlat))[:1]
    index_float = jnp.maximum(place, 1).astype(jnp.float32)
    log_steps = jnp.log((2.0 * index_float + 1.0) / (2.0 * index_float))
    picked_steps = jnp.where((place >= 1) & (place <= orders), log_steps, 0.0)
    cumulative = jnp.sum(picked_steps, axis=1, keepdims=True)
    diagonal_ref[...] = jnp.exp(
        0.5 * math.log(0.5) + 0.5 * cumulative + order_float * jnp.log(sines)
    )
    degree_all = iota(damping_ref.shape, 0).astype(jnp.float32)
    scaled = degree_all * (degree_all + 1.0) / ((nlat - 1.0) * nlat)
    damping_ref[...] = 1.0 / (1.0 + damping_strength * scaled * scaled) - 1.0

    nblk = list_ref.shape[-1]
    listed = jnp.broadcast_to(list_ref[0], (nblk, nblk)) == iota((nblk, nblk), 0)
    sunlit = listed & (iota((nblk, nblk), 1) < count_ref[0, 0])
    lit_column = jnp.sum(jnp.where(sunlit, 1.0, 0.0), axis=1, keepdims=True)
    lit_ref[...] = jnp.broadcast_to(lit_column, lit_ref.shape)
    per_row = nblk // rows
    wide, span, lanes = degrees.shape[0], degrees.shape[1] // rows, degrees.shape[2]

    def recurrence(base, index, pair):
        previous, earlier = pair
        degree = base + index
        degree_float = degree.astype(jnp.float32)
        square = degree_float * degree_float
        lower = degree_float - 1.0
        lower_square = lower * lower
        factor_now = jnp.sqrt((4.0 * square - 1.0) / jnp.maximum(square - order_square, 1.0))
        factor_back = jnp.sqrt(
            jnp.maximum(lower_square - order_square, 0.0)
            / jnp.maximum(4.0 * lower_square - 1.0, 1.0)
        )
        general = factor_now * (cosines * previous - factor_back * earlier)
        value = jnp.where(degree == orders, diagonal_ref[...], jnp.where(degree > orders, general, 0.0))
        place = pl.ds(pl.multiple_of(index * rows, rows), rows)
        for part in range(wide):
            degrees[part, place] = value[:, part * lanes : (part + 1) * lanes]
        return value, previous

    pair = (diagonal_ref[...] * 0.0, diagonal_ref[...] * 0.0)
    for base in range(0, nlat, span):
        pair = lax.fori_loop(0, span, functools.partial(recurrence, base), pair, unroll=4)

        @pl.loop(0, rows)
        def _(m):
            picked = jnp.concatenate(
                [degrees[part, pl.ds(m, span, stride=rows), :] for part in range(wide)], axis=1
            )
            analysis[m, base : base + span, :] = (picked * weights).astype(jnp.bfloat16)
            synthesis[m, :, base : base + span] = picked.T.astype(jnp.bfloat16)

    wt_in[...] = w_in_ref[...].astype(jnp.float32).T.astype(jnp.bfloat16)
    wt_mid[...] = w_mid_ref[...].astype(jnp.float32).T.astype(jnp.bfloat16)
    wt_out[...] = w_out_ref[...].astype(jnp.float32).T.astype(jnp.bfloat16)
    humid_load.wait()

    def network_row(j):
        profile = jnp.concatenate([grid[j].astype(jnp.bfloat16), humid[j]], axis=0)
        first = silu(dot(wt_in[...], profile, ((1,), (0,)))).astype(jnp.bfloat16)
        second = silu(dot(wt_mid[...], first, ((1,), (0,)))).astype(jnp.bfloat16)
        heating = dot(wt_out[...], second, ((1,), (0,))).astype(jnp.bfloat16).astype(jnp.float32)
        lit = jnp.concatenate(
            [lit_ref[pl.ds(j * per_row + k, 1), :] for k in range(per_row)], axis=1
        )
        grid[j] = grid[j] + jnp.where(lit > 0.5, heating, 0.0)

    early = rows // 2
    pl.loop(0, early, unroll=2)(network_row)

    for step in order[:-1]:
        waves[step].wait_recv()

    @pl.loop(0, rows, unroll=4)
    def _(m):
        place = pl.ds(pl.multiple_of(m * rows, rows), rows)
        fourier = by_wave[:, place, :].reshape(nlat, levels)
        spectral = dot(analysis[m], fourier, ((1,), (0,)))
        damped = (spectral * damping_ref[...]).astype(jnp.bfloat16)
        back = dot(synthesis[m], damped, ((1,), (0,)))
        doubled = jnp.where(me * rows + m == 0, 1.0, 2.0)
        to_lat[:, place, :] = (back * doubled).astype(jnp.bfloat16).reshape(lat_size, rows, levels)

    lats = {}
    for step in order[:-1]:
        lats[step] = pltpu.make_async_remote_copy(
            src_ref=to_lat.at[owner(step)],
            dst_ref=by_lat.at[me],
            send_sem=lat_send.at[step],
            recv_sem=lat_recv.at[step],
            device_id={"lat": owner(step)},
            device_id_type=MESH,
        )
        lats[step].start()
    by_lat[me] = to_lat[me]

    pl.loop(early, rows, unroll=2)(network_row)
    store = pltpu.make_async_copy(grid, out_ref, out_sem)
    store.start()

    for step in order[:-1]:
        waves[step].wait_send()
    for step in order:
        pairs[step].wait_send()

    shares = {}
    arrival = [0] + order[:-1][::-1]
    for step in arrival:
        if step:
            lats[step].wait_recv()
        origin = source(step)
        shares[step] = pltpu.make_async_remote_copy(
            src_ref=by_lat.at[origin],
            dst_ref=sibling_part.at[origin],
            send_sem=share_send.at[step],
            recv_sem=share_recv.at[step],
            device_id={"lev": sibling},
            device_id_type=MESH,
        )
        shares[step].start()
        partial[0, chunk_rows(origin)] = by_lat[origin].astype(jnp.float32)
    for step in arrival:
        origin = source(step)
        shares[step].wait_recv()
        partial[1, chunk_rows(origin)] = sibling_part[origin].astype(jnp.float32)

    for j in range(rows):
        for part in range(2):
            back_ref[j, part * nlat : (part + 1) * nlat, :] = partial[
                part, pl.ds(j, nlat, stride=rows), :
            ].astype(jnp.bfloat16)

    for step in order[:-1]:
        lats[step].wait_send()
    for step in arrival:
        shares[step].wait_send()
    store.wait()


def inverse_kernel(warm_ref, back_ref, table_ref, out_ref):
    rows, levels, lons = out_ref.shape
    both = jnp.concatenate([back_ref[row] for row in range(rows)], axis=1)
    increment = dot(both, table_ref[...], ((0,), (0,)))
    out_ref[...] = warm_ref[...] + increment.reshape(rows, levels, lons)


def local(state, humidity, sun_list, sun_count, w_in, w_mid, w_out):
    rows, levels, half_lon = state.shape
    per_row = half_lon // BLOCK
    nblk = rows * per_row
    lat_size = lax.axis_size("lat")
    lev_size = lax.axis_size("lev")
    nlat = rows * lat_size
    chunk = rows * rows
    span = min(nlat, 128)
    vmem = pl.BlockSpec(memory_space=pltpu.VMEM)
    hbm = pl.BlockSpec(memory_space=pl.ANY)
    dma = pltpu.SemaphoreType.DMA
    low = jnp.bfloat16
    smem = pl.BlockSpec(memory_space=pltpu.SMEM)
    table_shape = (2 * nlat, half_lon)
    back_shape = (rows, 2 * nlat, levels)
    warm, back, table = pl.pallas_call(
        functools.partial(kernel, lat_size, lev_size),
        out_shape=(
            jax.ShapeDtypeStruct(state.shape, jnp.float32),
            jax.ShapeDtypeStruct(back_shape, low),
            jax.ShapeDtypeStruct(table_shape, low),
        ),
        in_specs=[smem] + [vmem] * 4 + [hbm] * 2,
        out_specs=(hbm, vmem, vmem),
        scratch_shapes=[
            pltpu.VMEM(state.shape, jnp.float32),
            pltpu.VMEM(state.shape, low),
            pltpu.VMEM((2, nlat * rows, levels), jnp.float32),
            pltpu.VMEM((nlat * rows, levels), jnp.float32),
            pltpu.VMEM((nlat * rows, levels), low),
            pltpu.VMEM((lat_size, chunk, levels), low),
            pltpu.VMEM((rows, nlat), jnp.float32),
            pltpu.VMEM((nlat, levels), jnp.float32),
            pltpu.VMEM((nblk, BLOCK), jnp.float32),
            pltpu.VMEM((nlat // span, span * rows, span), jnp.float32),
            pltpu.VMEM((rows, nlat, nlat), low),
            pltpu.VMEM((rows, nlat, nlat), low),
            pltpu.VMEM((lat_size, chunk, levels), low),
            pltpu.VMEM((lat_size, chunk, levels), low),
            pltpu.VMEM((lat_size, chunk, levels), low),
            pltpu.VMEM(w_in.shape[::-1], low),
            pltpu.VMEM(w_mid.shape[::-1], low),
            pltpu.VMEM(w_out.shape[::-1], low),
            dma((rows,)),
            dma,
            dma,
        ]
        + [dma((lat_size,))] * 8,
        compiler_params=pltpu.CompilerParams(
            collective_id=0, has_side_effects=True, vmem_limit_bytes=(59 if nlat > 128 else 24) * MIB
        ),
    )(sun_count, sun_list, w_in, w_mid, w_out, state, humidity)
    tall = 2
    return pl.pallas_call(
        inverse_kernel,
        grid=(rows // tall,),
        out_shape=jax.ShapeDtypeStruct(state.shape, jnp.float32),
        in_specs=[
            pl.BlockSpec((tall, levels, half_lon), lambda i: (i, 0, 0)),
            pl.BlockSpec((tall, 2 * nlat, levels), lambda i: (i, 0, 0)),
            pl.BlockSpec(table_shape, lambda i: (0, 0)),
        ],
        out_specs=pl.BlockSpec((tall, levels, half_lon), lambda i: (i, 0, 0)),
        compiler_params=pltpu.CompilerParams(vmem_limit_bytes=16 * MIB),
    )(warm, back, table)


def solution(mesh):
    return jax.shard_map(
        local,
        mesh=mesh,
        in_specs=(
            P(("groups", "lat"), None, "lev"),
            P(("groups", "lat"), None, "lev"),
            P(("groups", "lat"), "lev", None),
            P(("groups", "lat"), "lev"),
            P(),
            P(),
            P(),
        ),
        out_specs=P(("groups", "lat"), None, "lev"),
        check_vma=False,
    )
```

```python
import functools
import math

import jax
import jax.numpy as jnp
from jax import lax
from jax.experimental import pallas as pl
from jax.experimental.pallas import tpu as pltpu
from jax.sharding import PartitionSpec as P

BLOCK = 128
MESH = pl.DeviceIdType.MESH
MIB = 2**20

damping_strength = 10.0


def sine(angle):
    square = angle * angle
    series = 1.6059044e-10
    for term in (-2.5052108e-8, 2.7557319e-6, -1.9841270e-4, 8.3333333e-3, -0.16666667):
        series = series * square + term
    return angle + angle * square * series


def iota(shape, dimension):
    return lax.broadcasted_iota(jnp.int32, shape, dimension)


def silu(value):
    half = 0.5 * value
    return half + half * jnp.tanh(half)


def dot(left, right, contract):
    return lax.dot_general(left, right, (contract, ((), ())), preferred_element_type=jnp.float32)


def kernel(
    lat_size,
    lev_size,
    count_ref,
    list_ref,
    w_in_ref,
    w_mid_ref,
    w_out_ref,
    state_ref,
    humidity_ref,
    out_ref,
    back_ref,
    table_ref,
    grid,
    humid,
    partial,
    sibling_rows,
    from_sibling,
    to_wave,
    by_wave,
    diagonal_ref,
    damping_ref,
    lit_ref,
    degrees,
    analysis,
    synthesis,
    to_lat,
    by_lat,
    sibling_part,
    wt_in,
    wt_mid,
    wt_out,
    w_in_held,
    w_mid_held,
    w_out_held,
    state_sem,
    humid_sem,
    weight_sem,
    out_sem,
    pair_send,
    pair_recv,
    wave_send,
    wave_recv,
    lat_send,
    lat_recv,
    share_send,
    share_recv,
):
    rows, levels, lons = grid.shape
    nlat = lat_size * rows
    chunk = rows * rows
    me = lax.axis_index("lat")
    sibling = 1 - lax.axis_index("lev")

    loads = [
        pltpu.make_async_copy(state_ref.at[j], grid.at[j], state_sem.at[j]) for j in range(rows)
    ]
    for load in loads:
        load.start()
    humid_load = pltpu.make_async_copy(humidity_ref, humid, humid_sem)
    weight_loads = [
        pltpu.make_async_copy(source_ref, held, weight_sem.at[index])
        for index, (source_ref, held) in enumerate(
            ((w_in_ref, w_in_held), (w_mid_ref, w_mid_held), (w_out_ref, w_out_held))
        )
    ]

    barrier = pltpu.get_barrier_semaphore()
    for step in range(1, lat_size):
        pl.semaphore_signal(
            barrier,
            inc=1,
            device_id={"lat": lax.rem(me + step, lat_size)},
            device_id_type=MESH,
        )
    pl.semaphore_signal(barrier, inc=1, device_id={"lev": sibling}, device_id_type=MESH)

    lev = lax.axis_index("lev")
    nlon = lons * lev_size
    strip = min(nlat, 128)
    for half in range(2):
        turn = jnp.where(lev == half, 0, nlon // 4)
        for base in range(0, nlat, strip):
            wavenumber = base + iota((strip, lons), 0)
            longitude = lev * lons + iota((strip, lons), 1)
            turned = longitude * wavenumber + turn
            phase = turned & (nlon - 1) if nlon & (nlon - 1) == 0 else turned % nlon
            fold = nlon // 4 - jnp.minimum(phase, nlon - phase)
            values = sine(fold.astype(jnp.float32) * (2.0 * math.pi / nlon))
            place = half * nlat + base
            table_ref[place : place + strip, :] = values.astype(jnp.bfloat16)

    pairs = []
    for j in range(0, rows, 2):
        loads[j].wait()
        loads[j + 1].wait()
        two = grid[j : j + 2].astype(jnp.bfloat16).reshape(2 * levels, lons)
        sums = dot(table_ref[...], two, ((1,), (1,))) * (1.0 / nlon)
        partial[1, j * nlat : (j + 1) * nlat] = sums[:nlat, :levels]
        partial[1, (j + 1) * nlat : (j + 2) * nlat] = sums[:nlat, levels:]
        sibling_rows[j : j + 2] = jnp.stack([sums[nlat:, :levels], sums[nlat:, levels:]])
        if j == 0:
            pl.semaphore_wait(barrier, lat_size)
        pair = pltpu.make_async_remote_copy(
            src_ref=sibling_rows.at[pl.ds(j, 2)],
            dst_ref=from_sibling.at[pl.ds(j, 2)],
            send_sem=pair_send.at[j // 2],
            recv_sem=pair_recv.at[j // 2],
            device_id={"lev": sibling},
            device_id_type=MESH,
        )
        pair.start()
        pairs.append(pair)

    humid_load.start()
    for load in weight_loads:
        load.start()
    for j in range(0, rows, 2):
        pairs[j // 2].wait_recv()
        for row in range(j, j + 2):
            whole = partial[1, row * nlat : (row + 1) * nlat] + from_sibling[row]
            partial[0, pl.ds(row, nlat, stride=rows), :] = whole

    middle = lat_size // 2
    order = sorted(range(1, lat_size), key=lambda step: abs(step - middle)) + [0]

    def owner(step):
        return lax.rem(me + step, lat_size)

    def source(step):
        return lax.rem(me + lat_size - step, lat_size)

    def chunk_rows(index):
        return pl.ds(pl.multiple_of(index * chunk, chunk), chunk)

    waves = {}
    for step in order:
        place = chunk_rows(owner(step))
        whole = partial[0, place].astype(jnp.bfloat16)
        if step == 0:
            by_wave[me] = whole
            continue
        to_wave[place] = whole
        waves[step] = pltpu.make_async_remote_copy(
            src_ref=to_wave.at[place],
            dst_ref=by_wave.at[me],
            send_sem=wave_send.at[step],
            recv_sem=wave_recv.at[step],
            device_id={"lat": owner(step)},
            device_id_type=MESH,
        )
        waves[step].start()

    orders = me * rows + iota(diagonal_ref.shape, 0)
    order_float = orders.astype(jnp.float32)
    order_square = order_float * order_float
    place = iota(diagonal_ref.shape, 1)
    cosines = sine((nlat - 1 - 2 * place).astype(jnp.float32) * (0.5 * math.pi / nlat))
    near = jnp.minimum(2 * place + 1, 2 * nlat - 1 - 2 * place).astype(jnp.float32)
    sines = sine(near * (0.5 * math.pi / nlat))
    weights = (sines * (math.pi / nlat))[:1]
    index_float = jnp.maximum(place, 1).astype(jnp.float32)
    log_steps = jnp.log((2.0 * index_float + 1.0) / (2.0 * index_float))
    picked_steps = jnp.where((place >= 1) & (place <= orders), log_steps, 0.0)
    cumulative = jnp.sum(picked_steps, axis=1, keepdims=True)
    diagonal_ref[...] = jnp.exp(
        0.5 * math.log(0.5) + 0.5 * cumulative + order_float * jnp.log(sines)
    )
    degree_all = iota(damping_ref.shape, 0).astype(jnp.float32)
    scaled = degree_all * (degree_all + 1.0) / ((nlat - 1.0) * nlat)
    damping_ref[...] = 1.0 / (1.0 + damping_strength * scaled * scaled) - 1.0

    nblk = list_ref.shape[-1]
    listed = jnp.broadcast_to(list_ref[0], (nblk, nblk)) == iota((nblk, nblk), 0)
    sunlit = listed & (iota((nblk, nblk), 1) < count_ref[0, 0])
    lit_column = jnp.sum(jnp.where(sunlit, 1.0, 0.0), axis=1, keepdims=True)
    lit_ref[...] = jnp.broadcast_to(lit_column, lit_ref.shape)
    per_row = nblk // rows
    wide, span, lanes = degrees.shape[0], degrees.shape[1] // rows, degrees.shape[2]

    def recurrence(base, index, pair):
        previous, earlier = pair
        degree = base + index
        degree_float = degree.astype(jnp.float32)
        square = degree_float * degree_float
        lower = degree_float - 1.0
        lower_square = lower * lower
        factor_now = jnp.sqrt((4.0 * square - 1.0) / jnp.maximum(square - order_square, 1.0))
        factor_back = jnp.sqrt(
            jnp.maximum(lower_square - order_square, 0.0)
            / jnp.maximum(4.0 * lower_square - 1.0, 1.0)
        )
        general = factor_now * (cosines * previous - factor_back * earlier)
        value = jnp.where(degree == orders, diagonal_ref[...], jnp.where(degree > orders, general, 0.0))
        place = pl.ds(pl.multiple_of(index * rows, rows), rows)
        for part in range(wide):
            degrees[part, place] = value[:, part * lanes : (part + 1) * lanes]
        return value, previous

    pair = (diagonal_ref[...] * 0.0, diagonal_ref[...] * 0.0)
    for base in range(0, nlat, span):
        pair = lax.fori_loop(0, span, functools.partial(recurrence, base), pair, unroll=4)

        @pl.loop(0, rows)
        def _(m):
            picked = jnp.concatenate(
                [degrees[part, pl.ds(m, span, stride=rows), :] for part in range(wide)], axis=1
            )
            analysis[m, base : base + span, :] = (picked * weights).astype(jnp.bfloat16)
            synthesis[m, :, base : base + span] = picked.T.astype(jnp.bfloat16)

    for load in weight_loads:
        load.wait()
    wt_in[...] = w_in_held[...].astype(jnp.float32).T.astype(jnp.bfloat16)
    wt_mid[...] = w_mid_held[...].astype(jnp.float32).T.astype(jnp.bfloat16)
    wt_out[...] = w_out_held[...].astype(jnp.float32).T.astype(jnp.bfloat16)
    humid_load.wait()

    def network_row(j):
        profile = jnp.concatenate([grid[j].astype(jnp.bfloat16), humid[j]], axis=0)
        first = silu(dot(wt_in[...], profile, ((1,), (0,)))).astype(jnp.bfloat16)
        second = silu(dot(wt_mid[...], first, ((1,), (0,)))).astype(jnp.bfloat16)
        heating = dot(wt_out[...], second, ((1,), (0,))).astype(jnp.bfloat16).astype(jnp.float32)
        lit = jnp.concatenate(
            [lit_ref[pl.ds(j * per_row + k, 1), :] for k in range(per_row)], axis=1
        )
        grid[j] = grid[j] + jnp.where(lit > 0.5, heating, 0.0)

    early = rows // 2
    pl.loop(0, early, unroll=2)(network_row)

    for step in order[:-1]:
        waves[step].wait_recv()

    @pl.loop(0, rows, unroll=4)
    def _(m):
        place = pl.ds(pl.multiple_of(m * rows, rows), rows)
        fourier = by_wave[:, place, :].reshape(nlat, levels)
        spectral = dot(analysis[m], fourier, ((1,), (0,)))
        damped = (spectral * damping_ref[...]).astype(jnp.bfloat16)
        back = dot(synthesis[m], damped, ((1,), (0,)))
        doubled = jnp.where(me * rows + m == 0, 1.0, 2.0)
        to_lat[:, place, :] = (back * doubled).astype(jnp.bfloat16).reshape(lat_size, rows, levels)

    lats = {}
    for step in order[:-1]:
        lats[step] = pltpu.make_async_remote_copy(
            src_ref=to_lat.at[owner(step)],
            dst_ref=by_lat.at[me],
            send_sem=lat_send.at[step],
            recv_sem=lat_recv.at[step],
            device_id={"lat": owner(step)},
            device_id_type=MESH,
        )
        lats[step].start()
    by_lat[me] = to_lat[me]

    pl.loop(early, rows, unroll=2)(network_row)
    store = pltpu.make_async_copy(grid, out_ref, out_sem)
    store.start()

    for step in order[:-1]:
        waves[step].wait_send()
    for pair in pairs:
        pair.wait_send()

    shares = {}
    arrival = [0] + order[:-1][::-1]
    for step in arrival:
        if step:
            lats[step].wait_recv()
        origin = source(step)
        shares[step] = pltpu.make_async_remote_copy(
            src_ref=by_lat.at[origin],
            dst_ref=sibling_part.at[origin],
            send_sem=share_send.at[step],
            recv_sem=share_recv.at[step],
            device_id={"lev": sibling},
            device_id_type=MESH,
        )
        shares[step].start()
        partial[0, chunk_rows(origin)] = by_lat[origin].astype(jnp.float32)
    for step in arrival:
        origin = source(step)
        shares[step].wait_recv()
        partial[1, chunk_rows(origin)] = sibling_part[origin].astype(jnp.float32)

    for j in range(rows):
        for part in range(2):
            back_ref[j, part * nlat : (part + 1) * nlat, :] = partial[
                part, pl.ds(j, nlat, stride=rows), :
            ].astype(jnp.bfloat16)

    for step in order[:-1]:
        lats[step].wait_send()
    for step in arrival:
        shares[step].wait_send()
    store.wait()


def inverse_kernel(warm_ref, back_ref, table_ref, out_ref):
    rows, levels, lons = out_ref.shape
    both = jnp.concatenate([back_ref[row] for row in range(rows)], axis=1)
    increment = dot(both, table_ref[...], ((0,), (0,)))
    out_ref[...] = warm_ref[...] + increment.reshape(rows, levels, lons)


def local(state, humidity, sun_list, sun_count, w_in, w_mid, w_out):
    rows, levels, half_lon = state.shape
    per_row = half_lon // BLOCK
    nblk = rows * per_row
    lat_size = lax.axis_size("lat")
    lev_size = lax.axis_size("lev")
    nlat = rows * lat_size
    chunk = rows * rows
    span = min(nlat, 128)
    vmem = pl.BlockSpec(memory_space=pltpu.VMEM)
    hbm = pl.BlockSpec(memory_space=pl.ANY)
    dma = pltpu.SemaphoreType.DMA
    low = jnp.bfloat16
    smem = pl.BlockSpec(memory_space=pltpu.SMEM)
    table_shape = (2 * nlat, half_lon)
    back_shape = (rows, 2 * nlat, levels)
    warm, back, table = pl.pallas_call(
        functools.partial(kernel, lat_size, lev_size),
        out_shape=(
            jax.ShapeDtypeStruct(state.shape, jnp.float32),
            jax.ShapeDtypeStruct(back_shape, low),
            jax.ShapeDtypeStruct(table_shape, low),
        ),
        in_specs=[smem, vmem] + [hbm] * 5,
        out_specs=(hbm, vmem, vmem),
        scratch_shapes=[
            pltpu.VMEM(state.shape, jnp.float32),
            pltpu.VMEM(state.shape, low),
            pltpu.VMEM((2, nlat * rows, levels), jnp.float32),
            pltpu.VMEM((rows, nlat, levels), jnp.float32),
            pltpu.VMEM((rows, nlat, levels), jnp.float32),
            pltpu.VMEM((nlat * rows, levels), low),
            pltpu.VMEM((lat_size, chunk, levels), low),
            pltpu.VMEM((rows, nlat), jnp.float32),
            pltpu.VMEM((nlat, levels), jnp.float32),
            pltpu.VMEM((nblk, BLOCK), jnp.float32),
            pltpu.VMEM((nlat // span, span * rows, span), jnp.float32),
            pltpu.VMEM((rows, nlat, nlat), low),
            pltpu.VMEM((rows, nlat, nlat), low),
            pltpu.VMEM((lat_size, chunk, levels), low),
            pltpu.VMEM((lat_size, chunk, levels), low),
            pltpu.VMEM((lat_size, chunk, levels), low),
            pltpu.VMEM(w_in.shape[::-1], low),
            pltpu.VMEM(w_mid.shape[::-1], low),
            pltpu.VMEM(w_out.shape[::-1], low),
            pltpu.VMEM(w_in.shape, low),
            pltpu.VMEM(w_mid.shape, low),
            pltpu.VMEM(w_out.shape, low),
            dma((rows,)),
            dma,
            dma((3,)),
            dma,
        ]
        + [dma((rows // 2,))] * 2
        + [dma((lat_size,))] * 6,
        compiler_params=pltpu.CompilerParams(
            collective_id=0, has_side_effects=True, vmem_limit_bytes=59 * MIB
        ),
    )(sun_count, sun_list, w_in, w_mid, w_out, state, humidity)
    tall = 2
    return pl.pallas_call(
        inverse_kernel,
        grid=(rows // tall,),
        out_shape=jax.ShapeDtypeStruct(state.shape, jnp.float32),
        in_specs=[
            pl.BlockSpec((tall, levels, half_lon), lambda i: (i, 0, 0)),
            pl.BlockSpec((tall, 2 * nlat, levels), lambda i: (i, 0, 0)),
            pl.BlockSpec(table_shape, lambda i: (0, 0)),
        ],
        out_specs=pl.BlockSpec((tall, levels, half_lon), lambda i: (i, 0, 0)),
        compiler_params=pltpu.CompilerParams(vmem_limit_bytes=16 * MIB),
    )(warm, back, table)


def solution(mesh):
    return jax.shard_map(
        local,
        mesh=mesh,
        in_specs=(
            P(("groups", "lat"), None, "lev"),
            P(("groups", "lat"), None, "lev"),
            P(("groups", "lat"), "lev", None),
            P(("groups", "lat"), "lev"),
            P(),
            P(),
            P(),
        ),
        out_specs=P(("groups", "lat"), None, "lev"),
        check_vma=False,
    )
```

```python
import functools
import math

import jax
import jax.numpy as jnp
from jax import lax
from jax.experimental import pallas as pl
from jax.experimental.pallas import tpu as pltpu
from jax.sharding import PartitionSpec as P

BLOCK = 128
MESH = pl.DeviceIdType.MESH
MIB = 2**20

damping_strength = 10.0


def sine(angle):
    square = angle * angle
    series = 1.6059044e-10
    for term in (-2.5052108e-8, 2.7557319e-6, -1.9841270e-4, 8.3333333e-3, -0.16666667):
        series = series * square + term
    return angle + angle * square * series


def iota(shape, dimension):
    return lax.broadcasted_iota(jnp.int32, shape, dimension)


def silu(value):
    half = 0.5 * value
    return half + half * jnp.tanh(half)


def dot(left, right, contract):
    return lax.dot_general(left, right, (contract, ((), ())), preferred_element_type=jnp.float32)


def kernel(
    lat_size,
    lev_size,
    count_ref,
    list_ref,
    w_in_ref,
    w_mid_ref,
    w_out_ref,
    state_ref,
    humidity_ref,
    out_ref,
    back_ref,
    table_ref,
    grid,
    humid,
    partial,
    sibling_rows,
    from_sibling,
    to_wave,
    by_wave,
    diagonal_ref,
    damping_ref,
    lit_ref,
    degrees,
    analysis,
    synthesis,
    to_lat,
    by_lat,
    sibling_part,
    wt_in,
    wt_mid,
    wt_out,
    w_in_held,
    w_mid_held,
    w_out_held,
    state_sem,
    humid_sem,
    weight_sem,
    out_sem,
    pair_send,
    pair_recv,
    wave_send,
    wave_recv,
    lat_send,
    lat_recv,
    share_send,
    share_recv,
):
    rows, levels, lons = grid.shape
    nlat = lat_size * rows
    chunk = rows * rows
    me = lax.axis_index("lat")
    sibling = 1 - lax.axis_index("lev")

    loads = [
        pltpu.make_async_copy(state_ref.at[j], grid.at[j], state_sem.at[j]) for j in range(rows)
    ]
    for load in loads:
        load.start()
    humid_load = pltpu.make_async_copy(humidity_ref, humid, humid_sem)
    weight_loads = [
        pltpu.make_async_copy(source_ref, held, weight_sem.at[index])
        for index, (source_ref, held) in enumerate(
            ((w_in_ref, w_in_held), (w_mid_ref, w_mid_held), (w_out_ref, w_out_held))
        )
    ]

    barrier = pltpu.get_barrier_semaphore()
    for step in range(1, lat_size):
        pl.semaphore_signal(
            barrier,
            inc=1,
            device_id={"lat": lax.rem(me + step, lat_size)},
            device_id_type=MESH,
        )
    pl.semaphore_signal(barrier, inc=1, device_id={"lev": sibling}, device_id_type=MESH)

    lev = lax.axis_index("lev")
    nlon = lons * lev_size
    strip = min(nlat, 128)
    for half in range(2):
        turn = jnp.where(lev == half, 0, nlon // 4)
        for base in range(0, nlat, strip):
            wavenumber = base + iota((strip, lons), 0)
            longitude = lev * lons + iota((strip, lons), 1)
            turned = longitude * wavenumber + turn
            phase = turned & (nlon - 1) if nlon & (nlon - 1) == 0 else turned % nlon
            fold = nlon // 4 - jnp.minimum(phase, nlon - phase)
            values = sine(fold.astype(jnp.float32) * (2.0 * math.pi / nlon))
            place = half * nlat + base
            table_ref[place : place + strip, :] = values.astype(jnp.bfloat16)

    pairs = []
    for j in range(0, rows, 2):
        loads[j].wait()
        loads[j + 1].wait()
        two = grid[j : j + 2].astype(jnp.bfloat16).reshape(2 * levels, lons)
        sums = dot(table_ref[...], two, ((1,), (1,))) * (1.0 / nlon)
        partial[1, j * nlat : (j + 1) * nlat] = sums[:nlat, :levels]
        partial[1, (j + 1) * nlat : (j + 2) * nlat] = sums[:nlat, levels:]
        sibling_rows[j : j + 2] = jnp.stack([sums[nlat:, :levels], sums[nlat:, levels:]])
        if j == 0:
            pl.semaphore_wait(barrier, lat_size)
        pair = pltpu.make_async_remote_copy(
            src_ref=sibling_rows.at[pl.ds(j, 2)],
            dst_ref=from_sibling.at[pl.ds(j, 2)],
            send_sem=pair_send.at[j // 2],
            recv_sem=pair_recv.at[j // 2],
            device_id={"lev": sibling},
            device_id_type=MESH,
        )
        pair.start()
        pairs.append(pair)

    humid_load.start()
    for load in weight_loads:
        load.start()
    for j in range(0, rows, 2):
        pairs[j // 2].wait_recv()
        for row in range(j, j + 2):
            whole = partial[1, row * nlat : (row + 1) * nlat] + from_sibling[row]
            partial[0, pl.ds(row, nlat, stride=rows), :] = whole

    middle = lat_size // 2
    order = sorted(range(1, lat_size), key=lambda step: abs(step - middle)) + [0]

    def owner(step):
        return lax.rem(me + step, lat_size)

    def source(step):
        return lax.rem(me + lat_size - step, lat_size)

    def chunk_rows(index):
        return pl.ds(pl.multiple_of(index * chunk, chunk), chunk)

    waves = {}
    for step in order:
        place = chunk_rows(owner(step))
        whole = partial[0, place].astype(jnp.bfloat16)
        if step == 0:
            by_wave[me] = whole
            continue
        to_wave[place] = whole
        waves[step] = pltpu.make_async_remote_copy(
            src_ref=to_wave.at[place],
            dst_ref=by_wave.at[me],
            send_sem=wave_send.at[step],
            recv_sem=wave_recv.at[step],
            device_id={"lat": owner(step)},
            device_id_type=MESH,
        )
        waves[step].start()

    orders = me * rows + iota(diagonal_ref.shape, 0)
    order_float = orders.astype(jnp.float32)
    order_square = order_float * order_float
    place = iota(diagonal_ref.shape, 1)
    cosines = sine((nlat - 1 - 2 * place).astype(jnp.float32) * (0.5 * math.pi / nlat))
    near = jnp.minimum(2 * place + 1, 2 * nlat - 1 - 2 * place).astype(jnp.float32)
    sines = sine(near * (0.5 * math.pi / nlat))
    weights = (sines * (math.pi / nlat))[:1]
    index_float = jnp.maximum(place, 1).astype(jnp.float32)
    log_steps = jnp.log((2.0 * index_float + 1.0) / (2.0 * index_float))
    picked_steps = jnp.where((place >= 1) & (place <= orders), log_steps, 0.0)
    cumulative = jnp.sum(picked_steps, axis=1, keepdims=True)
    diagonal_ref[...] = jnp.exp(
        0.5 * math.log(0.5) + 0.5 * cumulative + order_float * jnp.log(sines)
    )
    degree_all = iota(damping_ref.shape, 0).astype(jnp.float32)
    scaled = degree_all * (degree_all + 1.0) / ((nlat - 1.0) * nlat)
    damping_ref[...] = 1.0 / (1.0 + damping_strength * scaled * scaled) - 1.0

    nblk = list_ref.shape[-1]
    listed = jnp.broadcast_to(list_ref[0], (nblk, nblk)) == iota((nblk, nblk), 0)
    sunlit = listed & (iota((nblk, nblk), 1) < count_ref[0, 0])
    lit_column = jnp.sum(jnp.where(sunlit, 1.0, 0.0), axis=1, keepdims=True)
    lit_ref[...] = jnp.broadcast_to(lit_column, lit_ref.shape)
    per_row = nblk // rows
    wide, span, lanes = degrees.shape[0], degrees.shape[1] // rows, degrees.shape[2]

    def recurrence(base, index, pair):
        previous, earlier = pair
        degree = base + index
        degree_float = degree.astype(jnp.float32)
        square = degree_float * degree_float
        lower = degree_float - 1.0
        lower_square = lower * lower
        factor_now = jnp.sqrt((4.0 * square - 1.0) / jnp.maximum(square - order_square, 1.0))
        factor_back = jnp.sqrt(
            jnp.maximum(lower_square - order_square, 0.0)
            / jnp.maximum(4.0 * lower_square - 1.0, 1.0)
        )
        general = factor_now * (cosines * previous - factor_back * earlier)
        value = jnp.where(degree == orders, diagonal_ref[...], jnp.where(degree > orders, general, 0.0))
        place = pl.ds(pl.multiple_of(index * rows, rows), rows)
        for part in range(wide):
            degrees[part, place] = value[:, part * lanes : (part + 1) * lanes]
        return value, previous

    pair = (diagonal_ref[...] * 0.0, diagonal_ref[...] * 0.0)
    for base in range(0, nlat, span):
        pair = lax.fori_loop(0, span, functools.partial(recurrence, base), pair, unroll=4)

        @pl.loop(0, rows)
        def _(m):
            picked = jnp.concatenate(
                [degrees[part, pl.ds(m, span, stride=rows), :] for part in range(wide)], axis=1
            )
            analysis[m, base : base + span, :] = (picked * weights).astype(jnp.bfloat16)
            synthesis[m, :, base : base + span] = picked.T.astype(jnp.bfloat16)

    for load in weight_loads:
        load.wait()
    wt_in[...] = w_in_held[...].astype(jnp.float32).T.astype(jnp.bfloat16)
    wt_mid[...] = w_mid_held[...].astype(jnp.float32).T.astype(jnp.bfloat16)
    wt_out[...] = w_out_held[...].astype(jnp.float32).T.astype(jnp.bfloat16)
    humid_load.wait()

    def network_row(j):
        profile = jnp.concatenate([grid[j].astype(jnp.bfloat16), humid[j]], axis=0)
        first = silu(dot(wt_in[...], profile, ((1,), (0,)))).astype(jnp.bfloat16)
        second = silu(dot(wt_mid[...], first, ((1,), (0,)))).astype(jnp.bfloat16)
        heating = dot(wt_out[...], second, ((1,), (0,))).astype(jnp.bfloat16).astype(jnp.float32)
        lit = jnp.concatenate(
            [lit_ref[pl.ds(j * per_row + k, 1), :] for k in range(per_row)], axis=1
        )
        grid[j] = grid[j] + jnp.where(lit > 0.5, heating, 0.0)

    early = rows // 2
    pl.loop(0, early, unroll=2)(network_row)

    for step in order[:-1]:
        waves[step].wait_recv()

    @pl.loop(0, rows, unroll=4)
    def _(m):
        place = pl.ds(pl.multiple_of(m * rows, rows), rows)
        fourier = by_wave[:, place, :].reshape(nlat, levels)
        spectral = dot(analysis[m], fourier, ((1,), (0,)))
        damped = (spectral * damping_ref[...]).astype(jnp.bfloat16)
        back = dot(synthesis[m], damped, ((1,), (0,)))
        doubled = jnp.where(me * rows + m == 0, 1.0, 2.0)
        to_lat[:, place, :] = (back * doubled).astype(jnp.bfloat16).reshape(lat_size, rows, levels)

    lats = {}
    for step in order[:-1]:
        lats[step] = pltpu.make_async_remote_copy(
            src_ref=to_lat.at[owner(step)],
            dst_ref=by_lat.at[me],
            send_sem=lat_send.at[step],
            recv_sem=lat_recv.at[step],
            device_id={"lat": owner(step)},
            device_id_type=MESH,
        )
        lats[step].start()
    by_lat[me] = to_lat[me]

    pl.loop(early, rows, unroll=2)(network_row)
    store = pltpu.make_async_copy(grid, out_ref, out_sem)
    store.start()

    for step in order[:-1]:
        waves[step].wait_send()
    for pair in pairs:
        pair.wait_send()

    shares = {}
    arrival = [0] + order[:-1][::-1]
    for step in arrival:
        if step:
            lats[step].wait_recv()
        origin = source(step)
        shares[step] = pltpu.make_async_remote_copy(
            src_ref=by_lat.at[origin],
            dst_ref=sibling_part.at[origin],
            send_sem=share_send.at[step],
            recv_sem=share_recv.at[step],
            device_id={"lev": sibling},
            device_id_type=MESH,
        )
        shares[step].start()
        partial[0, chunk_rows(origin)] = by_lat[origin].astype(jnp.float32)
    for step in arrival:
        origin = source(step)
        shares[step].wait_recv()
        partial[1, chunk_rows(origin)] = sibling_part[origin].astype(jnp.float32)

    for j in range(rows):
        for part in range(2):
            back_ref[j, part * nlat : (part + 1) * nlat, :] = partial[
                part, pl.ds(j, nlat, stride=rows), :
            ].astype(jnp.bfloat16)

    for step in order[:-1]:
        lats[step].wait_send()
    for step in arrival:
        shares[step].wait_send()
    store.wait()


def inverse_kernel(warm_ref, back_ref, table_ref, out_ref):
    rows, levels, lons = out_ref.shape
    both = jnp.concatenate([back_ref[row] for row in range(rows)], axis=1)
    increment = dot(both, table_ref[...], ((0,), (0,)))
    out_ref[...] = warm_ref[...] + increment.reshape(rows, levels, lons)


def local(state, humidity, sun_list, sun_count, w_in, w_mid, w_out):
    rows, levels, half_lon = state.shape
    per_row = half_lon // BLOCK
    nblk = rows * per_row
    lat_size = lax.axis_size("lat")
    lev_size = lax.axis_size("lev")
    nlat = rows * lat_size
    chunk = rows * rows
    span = min(nlat, 128)
    vmem = pl.BlockSpec(memory_space=pltpu.VMEM)
    hbm = pl.BlockSpec(memory_space=pl.ANY)
    dma = pltpu.SemaphoreType.DMA
    low = jnp.bfloat16
    smem = pl.BlockSpec(memory_space=pltpu.SMEM)
    table_shape = (2 * nlat, half_lon)
    back_shape = (rows, 2 * nlat, levels)
    warm, back, table = pl.pallas_call(
        functools.partial(kernel, lat_size, lev_size),
        out_shape=(
            jax.ShapeDtypeStruct(state.shape, jnp.float32),
            jax.ShapeDtypeStruct(back_shape, low),
            jax.ShapeDtypeStruct(table_shape, low),
        ),
        in_specs=[smem, vmem] + [hbm] * 5,
        out_specs=(hbm, vmem, vmem),
        scratch_shapes=[
            pltpu.VMEM(state.shape, jnp.float32),
            pltpu.VMEM(state.shape, low),
            pltpu.VMEM((2, nlat * rows, levels), jnp.float32),
            pltpu.VMEM((rows, nlat, levels), jnp.float32),
            pltpu.VMEM((rows, nlat, levels), jnp.float32),
            pltpu.VMEM((nlat * rows, levels), low),
            pltpu.VMEM((lat_size, chunk, levels), low),
            pltpu.VMEM((rows, nlat), jnp.float32),
            pltpu.VMEM((nlat, levels), jnp.float32),
            pltpu.VMEM((nblk, BLOCK), jnp.float32),
            pltpu.VMEM((nlat // span, span * rows, span), jnp.float32),
            pltpu.VMEM((rows, nlat, nlat), low),
            pltpu.VMEM((rows, nlat, nlat), low),
            pltpu.VMEM((lat_size, chunk, levels), low),
            pltpu.VMEM((lat_size, chunk, levels), low),
            pltpu.VMEM((lat_size, chunk, levels), low),
            pltpu.VMEM(w_in.shape[::-1], low),
            pltpu.VMEM(w_mid.shape[::-1], low),
            pltpu.VMEM(w_out.shape[::-1], low),
            pltpu.VMEM(w_in.shape, low),
            pltpu.VMEM(w_mid.shape, low),
            pltpu.VMEM(w_out.shape, low),
            dma((rows,)),
            dma,
            dma((3,)),
            dma,
        ]
        + [dma((rows // 2,))] * 2
        + [dma((lat_size,))] * 6,
        compiler_params=pltpu.CompilerParams(
            collective_id=0, has_side_effects=True, vmem_limit_bytes=59 * MIB
        ),
    )(sun_count, sun_list, w_in, w_mid, w_out, state, humidity)
    tall = 2
    return pl.pallas_call(
        inverse_kernel,
        grid=(rows // tall,),
        out_shape=jax.ShapeDtypeStruct(state.shape, jnp.float32),
        in_specs=[
            pl.BlockSpec((tall, levels, half_lon), lambda i: (i, 0, 0)),
            pl.BlockSpec((tall, 2 * nlat, levels), lambda i: (i, 0, 0)),
            pl.BlockSpec(table_shape, lambda i: (0, 0)),
        ],
        out_specs=pl.BlockSpec((tall, levels, half_lon), lambda i: (i, 0, 0)),
        compiler_params=pltpu.CompilerParams(vmem_limit_bytes=59 * MIB),
    )(warm, back, table)


def solution(mesh):
    return jax.shard_map(
        local,
        mesh=mesh,
        in_specs=(
            P(("groups", "lat"), None, "lev"),
            P(("groups", "lat"), None, "lev"),
            P(("groups", "lat"), "lev", None),
            P(("groups", "lat"), "lev"),
            P(),
            P(),
            P(),
        ),
        out_specs=P(("groups", "lat"), None, "lev"),
        check_vma=False,
    )
```
